1024 devices in a mesh: rows: 64 (over y, x, core), cols: 16 (over z).
Axes of the slice: x: 4, y: 8, z: 16, core: 2. Of those that a mesh axis runs over, the one named last changes fastest.
Arguments:
- fine_blocks: float32 [768, 7, 128, 128], P('rows'), may hold values from -0.5 to 0.5
- block_cols: int32 [768, 7], P('rows'), may hold values from 0 to 139, as said below
- row_length: int32 [768], P('rows'), may hold values from 4 to 7, as said below
- prolong: float32 [768, 2, 128, 128], P('rows', None, 'cols'), may hold values from -1.8 to 1.8
- aggregates: int32 [768, 2], P('rows'), may hold values from 0 to 191, as said below
- coarse_slot: int32 [768, 2, 7, 2], P('rows'), may hold values from 0 to 7
- send_plan: int32 [64, 64, 2], P('rows'), may hold values from -1 to 11, as said below
Outputs:
- coarse_blocks: float32 [192, 8, 128, 128], P('rows', None, 'cols')
The draws below stay inside these ranges and needn't reach their ends.
Inputs may be any that keep to these rules, and one draw needn't show every extreme that they name: send_plan[q, p, c] is a fine row local to device q that q sends to device p in slot c, or -1 for an empty slot; the rows one device sends to another are distinct; no device sends to itself; each device receives 2 rows from exactly one other device, and 25 rows in all. block_cols of a live slot names a local row (below 12) or a received row 12 + q * 2 + c with send_plan[q, p, c] >= 0; every received row is named by some live slot; slot 0 names the row itself; slots at or beyond row_length name 0. `row_length`: slot 0 is always live; on every device, some row has 7 live slots and some has 4. aggregates[i, 0] is a coarse row of the device that holds fine row i (device p holds coarse rows p * 3 to p * 3 + 2), and each of those is named by some fine row of p; aggregates[i, 1] is a coarse row of another device, and the fine rows of one device name coarse rows of any one other device at most 1 times, exactly 1 times for some.
All inputs are finite; a program needn't handle non-finite values.
Results may differ from the reference program's by a relative error of at most 0.0001.
Values sent between devices are 32-bit elements; how exact they have to be, the bound alone decides.
A program may use at most 32 MiB of HBM per device.

```python
import jax
import jax.numpy as jnp
from jax import lax

B = 128
FR = 12
KA = 7
KC = 8
PEERS = 64
CAP = 2
CR = 3
NF = 768
NC = 192
N_ROWS = 64


def layout(key):
    count_key, peer_key, row_key, order_key, pick_key = jax.random.split(key, 5)
    peer_count = PEERS
    base_share = 2 * FR // (peer_count - 1)
    remainder = 2 * FR % (peer_count - 1)
    ranking = jnp.arange(peer_count - 1)
    per_rank = base_share + (ranking < remainder).astype(jnp.int32) + (ranking == 0).astype(jnp.int32)
    orders = jax.vmap(lambda k: jax.random.permutation(k, peer_count - 1))(jax.random.split(peer_key, peer_count))
    partner = (jnp.arange(peer_count)[:, None] + 1 + orders) % peer_count
    counts = jnp.sum((partner[:, :, None] == jnp.arange(peer_count)[None, None, :]).astype(jnp.int32) * per_rank[None, :, None], axis=1)
    picked = jax.vmap(lambda k: jax.random.permutation(k, FR)[:CAP])(jax.random.split(row_key, peer_count * peer_count))
    picked = picked.reshape(peer_count, peer_count, CAP)
    used = jnp.arange(CAP)[None, None, :] < jnp.transpose(counts)[:, :, None]
    send_plan = jnp.where(used, picked, -1).astype(jnp.int32)
    lengths = jax.random.randint(count_key, (peer_count, FR), 4, KA + 1)
    lengths = lengths.at[:, 0].set(KA).at[:, 1].set(4)
    listed = 2 * FR + 1
    spots = FR * (KA - 1)

    def device_cols(device, key_order, key_pick):
        valid = (jnp.arange(CAP)[None, :] < counts[device][:, None]).reshape(-1)
        listing = jnp.argsort(jnp.where(valid, 0, 1).astype(jnp.int32), stable=True).astype(jnp.int32)
        live_spot = (jnp.arange(1, KA)[None, :] < lengths[device][:, None]).reshape(-1)
        shuffle = jax.random.permutation(key_order, spots)
        rank_shuffled = jnp.cumsum(live_spot[shuffle].astype(jnp.int32)) - 1
        rank = jnp.zeros((spots,), jnp.int32).at[shuffle].set(rank_shuffled.astype(jnp.int32))
        spare = jax.random.randint(key_pick, (spots,), 0, FR + listed)
        spare_col = jnp.where(spare < FR, spare, FR + listing[jnp.clip(spare - FR, 0, listed - 1)])
        ghost_col = FR + listing[jnp.clip(rank, 0, listed - 1)]
        column = jnp.where(rank < listed, ghost_col, spare_col)
        column = jnp.where(live_spot, column, 0).reshape(FR, KA - 1)
        return jnp.concatenate([jnp.arange(FR, dtype=jnp.int32)[:, None], column.astype(jnp.int32)], axis=1)
    columns = jax.vmap(device_cols)(jnp.arange(peer_count), jax.random.split(order_key, peer_count), jax.random.split(pick_key, peer_count))
    return (send_plan, lengths.reshape(NF).astype(jnp.int32), columns.reshape(NF, KA).astype(jnp.int32))


def draw_send_plan(key, part):
    return layout(key)[0]


def draw_row_length(key, part):
    return layout(key)[1]


def draw_block_cols(key, part):
    return layout(key)[2]


def draw_aggregates(key, part):
    key = jax.random.fold_in(key, 7)
    peer_count = PEERS

    def device_map(device, device_key):
        agg_key, extra_key, order_key, peer_key, local_key = jax.random.split(device_key, 5)
        chosen = jax.random.permutation(agg_key, FR)
        firsts = jnp.zeros((FR,), jnp.int32).at[chosen[:CR]].set(jnp.arange(CR, dtype=jnp.int32))
        marked = jnp.zeros((FR,), jnp.int32).at[chosen[:CR]].set(1)
        spread = jax.random.randint(extra_key, (FR,), 0, CR)
        first_col = device * CR + jnp.where(marked == 1, firsts, spread)
        row_order = jax.random.permutation(order_key, FR)
        rank = jnp.zeros((FR,), jnp.int32).at[row_order].set(jnp.arange(FR, dtype=jnp.int32))
        peer_order = jax.random.permutation(peer_key, peer_count - 1)
        target_dev = (device + 1 + peer_order[rank % (peer_count - 1)]) % peer_count
        second_col = target_dev * CR + jax.random.randint(local_key, (FR,), 0, CR)
        return jnp.stack([first_col, second_col], axis=1).astype(jnp.int32)
    mapped = jax.vmap(device_map)(jnp.arange(peer_count), jax.random.split(key, peer_count))
    return mapped.reshape(NF, 2).astype(jnp.int32)


def with_ends(array, key, least, largest):
    dims = array.shape
    spot = [jax.random.randint(jax.random.fold_in(key, axis), (), 0, dims[axis]) for axis in range(len(dims))]
    array = array.at[tuple(spot)].set(least)
    longest = dims.index(max(dims))
    spot[longest] = (spot[longest] + 1) % dims[longest]
    return array.at[tuple(spot)].set(largest)


def block_scale(rng, shape, shards, smallest, high):
    loudness, own = 1.0, jax.random.fold_in(rng, 6)
    for axis_at, parts in shards:
        draws = jnp.exp(jax.random.uniform(jax.random.fold_in(own, axis_at), (parts,), jnp.float32, smallest / len(shards), high / len(shards)))
        loudness = loudness * jnp.repeat(draws, shape[axis_at] // parts).reshape([-1 if axis == axis_at else 1 for axis in range(len(shape))])
    return loudness


def scatter_about(own_key, extent, scale, reach, shards=(), kind=jnp.bfloat16):
    result = scale * jax.random.normal(own_key, extent, jnp.float32)
    if shards:
        result = result * block_scale(own_key, extent, shards, -0.22, 0.18)
    return jnp.clip(result, -reach, reach).astype(kind)


def setup_inputs(seed: int = 0) -> dict:
    streams_of = jax.random.split(jax.random.key(seed), 8)
    fine_blocks = scatter_about(streams_of[0], (NF, KA, B, B), B ** -0.5, 0.5, ((0, 64),), jnp.float32)
    block_cols = draw_block_cols(jax.random.fold_in(streams_of[7], 71), 0)
    row_length = draw_row_length(jax.random.fold_in(streams_of[7], 71), 0)
    prolong = scatter_about(streams_of[3], (NF, 2, B, B), 0.3, 1.8, ((0, 64), (2, 16)), jnp.float32)
    aggregates = draw_aggregates(jax.random.fold_in(streams_of[7], 71), 0)
    coarse_slot = with_ends(jax.random.randint(streams_of[5], (NF, 2, KA, 2), 0, KC), jax.random.fold_in(streams_of[5], 1), 0, KC - 1).astype(jnp.int32)
    send_plan = draw_send_plan(jax.random.fold_in(streams_of[7], 71), 0)
    return {"fine_blocks": fine_blocks, "block_cols": block_cols, "row_length": row_length, "prolong": prolong, "aggregates": aggregates, "coarse_slot": coarse_slot, "send_plan": send_plan}


PRECISE = lax.Precision.HIGHEST


def reference(fine_blocks, block_cols, row_length, prolong, aggregates, coarse_slot, send_plan):
    owner_dev = (jnp.arange(NF) // FR).astype(jnp.int32)
    is_local = block_cols < FR
    offset = jnp.maximum(block_cols - FR, 0)
    source = jnp.clip(offset // CAP, 0, N_ROWS - 1).astype(jnp.int32)
    within = (offset % CAP).astype(jnp.int32)
    remote_row = send_plan[source, owner_dev[:, None], within]
    neighbour = jnp.where(is_local, owner_dev[:, None] * FR + block_cols, source * FR + jnp.maximum(remote_row, 0)).astype(jnp.int32)
    live_mask = (jnp.arange(KA)[None, :] < row_length[:, None]).astype(jnp.float32)
    target = (aggregates[:, :, None, None] * KC + coarse_slot).astype(jnp.int32)

    def one_row(total, item):
        blocks, columns, own_prolong, weight, places = item
        coupled = prolong[columns]
        applied = jnp.einsum("ksac,krc->ksar", coupled, blocks, precision=PRECISE)
        products = jnp.einsum("ksar,tbr->tksab", applied, own_prolong, precision=PRECISE)
        products = products * weight[None, :, None, None, None]
        total = total.at[places.reshape(-1)].add(products.reshape(-1, B, B))
        return total, None

    start = jnp.zeros((NC * KC, B, B), jnp.float32)
    total, _ = lax.scan(one_row, start, (fine_blocks, neighbour, prolong, live_mask, target))
    return total.reshape(NC, KC, B, B)
```

```python
import functools

import jax
import jax.numpy as jnp
from jax import lax
from jax.experimental import pallas as pl
from jax.experimental.pallas import tpu as pltpu
from jax.sharding import PartitionSpec as P

NX, NC = 4, 2
KC = 8
CR = 3
A8 = 8
LANES = 128
HALVES = 2
PARTS = 2
F32, BF16 = jnp.float32, jnp.bfloat16
NT = (((1,), (1,)), ((), ()))
NN = (((1,), (0,)), ((), ()))
MESH = pl.DeviceIdType.MESH


def split(v):
    high = v.astype(BF16)
    return high, (v - high.astype(F32)).astype(BF16)


def wide(v):
    high, low = split(v)
    return jnp.concatenate(
        [jnp.concatenate([high, high], axis=1), jnp.concatenate([low, jnp.zeros_like(low)], axis=1)], axis=0
    )


def steps_of(count, half):
    plus = count // 2 if half % 2 == 0 else count // 2 - 1
    return plus, count - 1 - plus


def ring_ids(count, halves):
    ids = {}
    for half in range(halves):
        for way, steps in zip((1, -1), steps_of(count, half)):
            for step in range(steps):
                ids[half, way, step] = len(ids)
    return ids


def kernel(
    dims, fine, prolong, tab, slots, pool_at, own_tag, out,
    blocks, cut, whole, column, tabs, tabs_s, picked, pool, applied, far, own, acc, crossed, running,
    local_sem, tab_send, tab_recv, z_send, z_recv, y_send, y_recv, g_send, g_recv,
    x_send, x_recv, c_send, c_recv, r_send, r_recv,
):
    NY, NZ, FR, KA = dims
    group = NX * NC
    per = NY + 1
    NB = NZ * A8
    EC = KC // HALVES
    hr = FR // HALVES
    pr = FR // PARTS
    row, z = lax.axis_index("rows"), lax.axis_index("cols")
    core, x, y = row % NC, (row // NC) % NX, row // group
    here = x * NC + core

    def rid(yy, xx, cc):
        return (yy * NX + xx) * NC + cc

    def copy(src, dst, send, recv, device):
        return pltpu.make_async_remote_copy(
            src_ref=src, dst_ref=dst, send_sem=send, recv_sem=recv, device_id=device, device_id_type=MESH
        )

    def z_dev(way):
        return (row, (z + way + NZ) % NZ)

    def y_dev(way):
        return (rid((y + way + NY) % NY, x, core), z)

    def x_dev(way):
        return (rid(y, (x + way + NX) % NX, core), z)

    def g_dev(o):
        return (rid(y, (x + o // NC) % NX, (core + o % NC) % NC), z)

    core_dev = (rid(y, x, (core + 1) % NC), z)

    load = pltpu.make_async_copy(fine, blocks, local_sem.at[0])
    load.start()

    barrier = pltpu.get_barrier_semaphore()
    partners = [z_dev(o) for o in sorted({1, NZ - 1})]
    partners += [y_dev(o) for o in range(1, NY)]
    partners += [g_dev(o) for o in range(1, group)]
    for device in partners:
        pl.semaphore_signal(barrier, inc=1, device_id=device, device_id_type=MESH)
    pl.semaphore_wait(barrier, len(partners))

    sent = []

    def go(c):
        c.start()
        sent.append(c)

    z_ids, y_ids, x_ids = ring_ids(NZ, HALVES), ring_ids(NY, HALVES), ring_ids(NX, HALVES)

    def rows_of(half):
        return pl.ds(half * hr, hr)

    def ring_send(buf, ids, send, recv, me, count, dev, half, way, step):
        at = (me - way * step + count) % count
        part = prolong.at[rows_of(half)] if step == 0 else buf.at[at, rows_of(half)]
        n = ids[half, way, step]
        go(copy(part, buf.at[at, rows_of(half)], send.at[n], recv.at[n], dev(way)))

    def ring_wait(buf, ids, send, recv, me, count, dev, half, way, step):
        at = (me - way * (step + 1) + 2 * count) % count
        part = buf.at[at, rows_of(half)]
        n = ids[half, way, step]
        copy(part, part, send.at[n], recv.at[n], dev(way)).wait_recv()

    zr = (whole, z_ids, z_send, z_recv, z, NZ, z_dev)
    yr = (column, y_ids, y_send, y_recv, y, NY, y_dev)

    def advance(ring, ids, step):
        for half in range(HALVES):
            for way in (1, -1):
                if (half, way, step) in ids:
                    ring_wait(*ring, half, way, step)
                    if (half, way, step + 1) in ids:
                        ring_send(*ring, half, way, step + 1)

    for half in range(HALVES):
        for way in (1, -1):
            if (half, way, 0) in y_ids:
                ring_send(*yr, half, way, 0)
    for o in range(1, NY):
        go(copy(tab, tabs.at[y], tab_send.at[o], tab_recv.at[o], y_dev(o)))
    for o in range(1, NX):
        go(copy(tab, tabs.at[NY + x], tab_send.at[NY + o], tab_recv.at[NY + o], x_dev(o)))
    for half in range(HALVES):
        for way in (1, -1):
            if (half, way, 0) in z_ids:
                ring_send(*zr, half, way, 0)

    mine = prolong[...]
    whole[z] = mine
    column[y] = mine
    pool[pl.ds(0, FR)] = mine
    tabs[y] = tab[...]
    tabs[NY + x] = tab[...]

    load.wait()

    @pl.loop(0, FR)
    def _(i):
        for k in range(KA):
            high, low = split(blocks[i * KA + k])
            cut[i * KA + k] = jnp.concatenate([high, low], axis=1)

    advance(yr, y_ids, 0)
    advance(zr, z_ids, 0)
    for o in range(1, NY):
        at = tabs.at[(y - o + NY) % NY]
        copy(at, at, tab_send.at[o], tab_recv.at[o], y_dev(o)).wait_recv()
    for o in range(1, NX):
        at = tabs.at[NY + (x - o + NX) % NX]
        copy(at, at, tab_send.at[NY + o], tab_recv.at[NY + o], x_dev(o)).wait_recv()
    to_scalar = pltpu.make_async_copy(tabs, tabs_s, local_sem.at[1])
    to_scalar.start()
    y_steps = NY // 2
    for step in range(1, y_steps):
        advance(yr, y_ids, step)
        advance(zr, z_ids, step)
    to_scalar.wait()

    def pick(o, put):
        dest = rid(y, (x + o // NC) % NX, (core + o % NC) % NC)
        second_y, second_row = 0, 0
        for yy in range(NY):
            put(yy, column[yy, tabs_s[yy, 0, dest]])
            extra = tabs_s[yy, 1, dest]
            second_y = jnp.where(extra > 0, yy, second_y)
            second_row = jnp.where(extra > 0, extra - 1, second_row)
        put(NY, column[second_y, second_row])

    for o in list(range(1, group)) + [0]:
        if o:
            def put(n, v, o=o):
                picked[o, n] = v
        else:
            def put(n, v):
                pool[FR + here * per + n] = v
        pick(o, put)
        if o:
            go(copy(
                picked.at[o], pool.at[pl.ds(FR + here * per, per)], g_send.at[o], g_recv.at[o], g_dev(o)
            ))

    z_steps = NZ // 2
    for step in range(y_steps, z_steps - 1):
        advance(zr, z_ids, step)
    for o in range(1, group):
        src = ((x - o // NC + NX) % NX) * NC + (core - o % NC + NC) % NC
        at = pool.at[pl.ds(FR + src * per, per)]
        copy(at, at, g_send.at[o], g_recv.at[o], g_dev(o)).wait_recv()
    if z_steps > y_steps:
        advance(zr, z_ids, z_steps - 1)

    r8 = lax.broadcasted_iota(jnp.int32, (KC * A8, LANES), 0)
    l8 = lax.broadcasted_iota(jnp.int32, (KC * A8, LANES), 1)
    same_a, slot_of = (r8 % A8) == (l8 % A8), r8 // A8

    def couple(i):
        for k in range(KA):
            lhs = wide(pool[pool_at[i * KA + k]].reshape(2 * A8, LANES))
            both = lax.dot_general(lhs, cut[i * KA + k], NT, preferred_element_type=F32)
            applied[i, 2 * A8 * k:2 * A8 * (k + 1)] = both[:2 * A8] + both[2 * A8:]
        applied[i, 2 * A8 * KA:] = jnp.zeros((LANES - 2 * A8 * KA, LANES), F32)

    def product(i, t):
        xh, xl = split(applied[i])
        where = jnp.where(same_a & (slots[i * 2 + t][None, :] == slot_of), 1.0, 0.0).astype(BF16)
        summed = lax.dot_general(
            jnp.concatenate([where, where], axis=1), jnp.concatenate([xh, xl], axis=0), NN,
            preferred_element_type=F32,
        )
        high, low = split(whole[:, i, t].reshape(NB, LANES))
        both = lax.dot_general(
            wide(summed), jnp.concatenate([high, low], axis=1), NT, preferred_element_type=F32
        )
        return (both[:KC * A8] + both[KC * A8:]).reshape(KC, A8, NB)

    def x_send_go(p, half, way, step):
        at = far.at[half, (x - way * step + NX) % NX, pl.ds(p * pr, pr)]
        n = p * len(x_ids) + x_ids[half, way, step]
        go(copy(at, at, x_send.at[n], x_recv.at[n], x_dev(way)))

    def x_wait(p, half, way, step):
        at = far.at[half, (x - way * (step + 1) + 2 * NX) % NX, pl.ds(p * pr, pr)]
        n = p * len(x_ids) + x_ids[half, way, step]
        copy(at, at, x_send.at[n], x_recv.at[n], x_dev(way)).wait_recv()

    def x_advance(p, step):
        for half in range(HALVES):
            for way in (1, -1):
                if (half, way, step) in x_ids:
                    x_wait(p, half, way, step)
                    if (half, way, step + 1) in x_ids:
                        x_send_go(p, half, way, step + 1)

    for p in range(PARTS):
        @pl.loop(p * pr, (p + 1) * pr)
        def _(i):
            couple(i)
            made = product(i, 1)
            for half in range(HALVES):
                far[half, x, i] = made[half * EC:(half + 1) * EC]

        for half in range(HALVES):
            for way in (1, -1):
                if (half, way, 0) in x_ids:
                    x_send_go(p, half, way, 0)

    own[...] = jnp.zeros_like(own)
    for p in range(PARTS):
        @pl.loop(p * pr, (p + 1) * pr)
        def _(i):
            made = product(i, 0)
            for c in range(CR):
                own[c] += made * jnp.where(own_tag[i] == c, 1.0, 0.0)

        x_advance(p, 0)
    for step in range(1, NX // 2):
        for p in range(PARTS):
            x_advance(p, step)

    for half in range(HALVES):
        for cc in range(NC):
            @pl.loop(0, NY)
            def _(yy):
                dest = rid(yy, x, cc)
                sums = [jnp.zeros((EC, A8, NB), F32) for _ in range(CR)]
                for xx in range(NX):
                    rows = far[half, xx, tabs_s[NY + xx, 2, dest]]
                    tag = tabs_s[NY + xx, 3, dest]
                    for c in range(CR):
                        sums[c] += rows * jnp.where(tag == c + 1, 1.0, 0.0)
                for c in range(CR):
                    acc[cc, half, yy, c] = sums[c]

        go(copy(acc.at[(core + 1) % NC, half], crossed.at[half], c_send.at[half], c_recv.at[half], core_dev))

    r_ids = ring_ids(NY, HALVES)

    def run(half, way, step):
        far_end = steps_of(NY, half)[0 if way == 1 else 1]
        dest = (y + way * (far_end - step) + 2 * NY) % NY
        n = r_ids[half, way, step]
        total = crossed[half, dest] + acc[core, half, dest]
        if step:
            total += running[r_ids[half, way, step - 1]]
        crossed[half, dest] = total
        go(copy(crossed.at[half, dest], running.at[n], r_send.at[n], r_recv.at[n], y_dev(way)))

    def run_wait(half, way, step):
        n = r_ids[half, way, step]
        copy(running.at[n], running.at[n], r_send.at[n], r_recv.at[n], y_dev(way)).wait_recv()

    for half in range(HALVES):
        at = crossed.at[half]
        copy(at, at, c_send.at[half], c_recv.at[half], core_dev).wait_recv()
        for way in (1, -1):
            if (half, way, 0) in r_ids:
                run(half, way, 0)
    for step in range(y_steps):
        for half in range(HALVES):
            for way in (1, -1):
                if (half, way, step) in r_ids:
                    run_wait(half, way, step)
                    if (half, way, step + 1) in r_ids:
                        run(half, way, step + 1)
    for half in range(HALVES):
        total = own[:, half * EC:(half + 1) * EC] + crossed[half, y] + acc[core, half, y]
        for way, steps in zip((1, -1), steps_of(NY, half)):
            if steps:
                total += running[r_ids[half, way, steps - 1]]
        out[:, half * EC:(half + 1) * EC] = total

    for c in sent:
        c.wait_send()


def per_device(fine_blocks, block_cols, row_length, prolong, aggregates, coarse_slot, send_plan):
    peers, NZ = lax.axis_size("rows"), lax.axis_size("cols")
    FR, KA = fine_blocks.shape[:2]
    group = NX * NC
    NY = peers // group
    per = NY + 1
    NB = NZ * A8
    EC = KC // HALVES

    plan = send_plan[0]
    first, second = plan[:, 0], plan[:, 1]
    main = jnp.where(first >= 0, first, jnp.maximum(second, 0))
    extra = jnp.where((first >= 0) & (second >= 0), second + 1, 0)
    target = aggregates[:, 1]
    hit = ((target // CR)[:, None] == jnp.arange(peers)[None, :]).astype(jnp.int32)
    held = jnp.sum(hit * jnp.arange(FR)[:, None], axis=0)
    tag = jnp.sum(hit * (target % CR + 1)[:, None], axis=0)
    tab = jnp.pad(jnp.stack([main, extra, held, tag]), ((0, 4), (0, LANES - peers))).astype(jnp.int32)

    live = jnp.arange(KA)[None, :] < row_length[:, None]
    cols, alive = block_cols.reshape(-1), live.reshape(-1)
    ghost = jnp.maximum(cols - FR, 0)
    source, at = ghost // 2, ghost % 2
    paired = jnp.any((cols[None, :] == cols[:, None] - 1) & alive[None, :], axis=1) & (at == 1)
    place = jnp.where(paired, NY, source // group)
    pool_at = jnp.where(cols < FR, cols, FR + (source % group) * per + place).astype(jnp.int32)

    slots = jnp.where(live[:, None, :, None], coarse_slot, -1).reshape(FR * 2, KA * 2)
    slots = jnp.repeat(slots, A8, axis=1)
    slots = jnp.pad(slots, ((0, 0), (0, LANES - slots.shape[1])), constant_values=-1)

    vm, sm = pl.BlockSpec(memory_space=pltpu.VMEM), pl.BlockSpec(memory_space=pltpu.SMEM)
    count_z, count_y = len(ring_ids(NZ, HALVES)), len(ring_ids(NY, HALVES))
    count_x = len(ring_ids(NX, HALVES)) * PARTS
    dma = pltpu.SemaphoreType.DMA
    return pl.pallas_call(
        functools.partial(kernel, (NY, NZ, FR, KA)),
        out_shape=jax.ShapeDtypeStruct((CR, KC, A8, NB), F32),
        in_specs=[pl.BlockSpec(memory_space=pl.ANY), vm, vm, vm, sm, sm],
        out_specs=vm,
        scratch_shapes=[
            pltpu.VMEM((FR * KA, LANES, LANES), F32),
            pltpu.VMEM((FR * KA, LANES, 2 * LANES), BF16),
            pltpu.VMEM((NZ, FR, 2, A8, LANES), F32),
            pltpu.VMEM((NY, FR, 2, A8, LANES), F32),
            pltpu.VMEM((NY + NX, 8, LANES), jnp.int32),
            pltpu.SMEM((NY + NX, 8, LANES), jnp.int32),
            pltpu.VMEM((group, per, 2, A8, LANES), F32),
            pltpu.VMEM((FR + group * per, 2, A8, LANES), F32),
            pltpu.VMEM((FR, LANES, LANES), F32),
            pltpu.VMEM((HALVES, NX, FR, EC, A8, NB), F32),
            pltpu.VMEM((CR, KC, A8, NB), F32),
            pltpu.VMEM((NC, HALVES, NY, CR, EC, A8, NB), F32),
            pltpu.VMEM((HALVES, NY, CR, EC, A8, NB), F32),
            pltpu.VMEM((count_y, CR, EC, A8, NB), F32),
            dma((2,)), dma((NY + NX,)), dma((NY + NX,)), dma((count_z,)), dma((count_z,)),
            dma((count_y,)), dma((count_y,)), dma((group,)), dma((group,)),
            dma((count_x,)), dma((count_x,)), dma((HALVES,)), dma((HALVES,)),
            dma((count_y,)), dma((count_y,)),
        ],
        compiler_params=pltpu.CompilerParams(
            collective_id=0, has_side_effects=True, vmem_limit_bytes=48 * 2**20
        ),
    )(
        fine_blocks.reshape(FR * KA, LANES, LANES), prolong, tab, slots, pool_at,
        (aggregates[:, 0] % CR).astype(jnp.int32),
    )


def solution(mesh):
    return jax.shard_map(
        per_device,
        mesh=mesh,
        in_specs=(
            P("rows", None, None, None),
            P("rows", None),
            P("rows"),
            P("rows", None, "cols", None),
            P("rows", None),
            P("rows", None, None, None),
            P("rows", None, None),
        ),
        out_specs=P("rows", None, "cols", None),
        check_vma=False,
    )
```

```python
import functools

import jax
import jax.numpy as jnp
from jax import lax
from jax.experimental import pallas as pl
from jax.experimental.pallas import tpu as pltpu
from jax.sharding import PartitionSpec as P

NX, NC = 4, 2
KC = 8
CR = 3
A8 = 8
LANES = 128
HALVES = 2
STAGES = 4
F32, BF16, I32 = jnp.float32, jnp.bfloat16, jnp.int32
NT = (((1,), (1,)), ((), ()))
NN = (((1,), (0,)), ((), ()))
MESH = pl.DeviceIdType.MESH


def split(v):
    high = v.astype(BF16)
    return high, (v - high.astype(F32)).astype(BF16)


def wide(v):
    high, low = split(v)
    return jnp.concatenate(
        [jnp.concatenate([high, high], axis=1), jnp.concatenate([low, jnp.zeros_like(low)], axis=1)], axis=0
    )


def steps_of(count, half):
    plus = count // 2 if half % 2 == 0 else count // 2 - 1
    return plus, count - 1 - plus


def ring_ids(count, halves):
    ids = {}
    for half in range(halves):
        for way, steps in zip((1, -1), steps_of(count, half)):
            for step in range(steps):
                ids[half, way, step] = len(ids)
    return ids


def kernel(
    dims, fine, prolong, cols, lengths, agg, coarse, plan, out,
    blocks, cut, whole, column, plans, plans_s, tabs, tabs_s, cols_s, lengths_s, agg_s, coarse_s,
    picked, pool, applied, wided, far_a, far_b, far_c, far_d, own, acc, crossed, running,
    local_sem, tab_send, tab_recv, z_send, z_recv, y_send, y_recv, g_send, g_recv,
    x_send, x_recv, c_send, c_recv, r_send, r_recv,
):
    NY, NZ, FR, KA = dims
    group = NX * NC
    per = NY + 1
    NB = NZ * A8
    EC = KC // STAGES
    hr = FR // HALVES
    y_steps, z_steps = NY // 2, NZ // 2
    far = (far_a, far_b, far_c, far_d)
    row, z = lax.axis_index("rows"), lax.axis_index("cols")
    core, x, y = row % NC, (row // NC) % NX, row // group
    here = x * NC + core

    def rid(yy, xx, cc):
        return (yy * NX + xx) * NC + cc

    def copy(src, dst, send, recv, device):
        return pltpu.make_async_remote_copy(
            src_ref=src, dst_ref=dst, send_sem=send, recv_sem=recv, device_id=device, device_id_type=MESH
        )

    def z_dev(way):
        return (row, (z + way + NZ) % NZ)

    def y_dev(way):
        return (rid((y + way + NY) % NY, x, core), z)

    def x_dev(way):
        return (rid(y, (x + way + NX) % NX, core), z)

    def g_dev(o):
        return (rid(y, (x + o // NC) % NX, (core + o % NC) % NC), z)

    core_dev = (rid(y, x, (core + 1) % NC), z)

    def bring(n, src, dst):
        c = pltpu.make_async_copy(src, dst, local_sem.at[n])
        c.start()
        return c

    got_prolong = bring(0, prolong, whole.at[z])
    got_plan = bring(1, plan, plans.at[y])
    got_agg = bring(2, agg, agg_s)
    got_cols = bring(3, cols, cols_s)
    got_lengths = bring(4, lengths, lengths_s)
    got_coarse = bring(5, coarse, coarse_s)
    got_fine = bring(6, fine, blocks)

    barrier = pltpu.get_barrier_semaphore()
    partners = [z_dev(o) for o in sorted({1, NZ - 1})]
    partners += [y_dev(o) for o in range(1, NY)]
    partners += [g_dev(o) for o in range(1, group)]
    for device in partners:
        pl.semaphore_signal(barrier, inc=1, device_id=device, device_id_type=MESH)
    got_prolong.wait()
    got_plan.wait()
    pl.semaphore_wait(barrier, len(partners))

    sent = []

    def go(c):
        c.start()
        sent.append(c)

    z_ids, y_ids = ring_ids(NZ, HALVES), ring_ids(NY, HALVES)

    def rows_of(half):
        return pl.ds(half * hr, hr)

    def ring_send(buf, ids, send, recv, me, count, dev, half, way, step):
        at = (me - way * step + count) % count
        part = whole.at[z, rows_of(half)] if step == 0 else buf.at[at, rows_of(half)]
        n = ids[half, way, step]
        go(copy(part, buf.at[at, rows_of(half)], send.at[n], recv.at[n], dev(way)))

    def ring_wait(buf, ids, send, recv, me, count, dev, half, way, step):
        at = (me - way * (step + 1) + 2 * count) % count
        part = buf.at[at, rows_of(half)]
        n = ids[half, way, step]
        copy(part, part, send.at[n], recv.at[n], dev(way)).wait_recv()

    zr = (whole, z_ids, z_send, z_recv, z, NZ, z_dev)
    yr = (column, y_ids, y_send, y_recv, y, NY, y_dev)

    def advance(ring, ids, step):
        for half in range(HALVES):
            for way in (1, -1):
                if (half, way, step) in ids:
                    ring_wait(*ring, half, way, step)
                    if (half, way, step + 1) in ids:
                        ring_send(*ring, half, way, step + 1)

    for half in range(HALVES):
        for way in (1, -1):
            if (half, way, 0) in y_ids:
                ring_send(*yr, half, way, 0)
            if (half, way, 0) in z_ids:
                ring_send(*zr, half, way, 0)
    for o in range(1, NY):
        go(copy(plans.at[y], plans.at[y], tab_send.at[o], tab_recv.at[o], y_dev(o)))
    column[y] = whole[z]
    pool[pl.ds(0, FR)] = whole[z]

    lane = lax.broadcasted_iota(I32, (8, LANES), 1)
    sub = lax.broadcasted_iota(I32, (8, LANES), 0)
    got_agg.wait()
    held = jnp.zeros((8, LANES), I32)
    tag = jnp.zeros((8, LANES), I32)
    for i in range(FR):
        off = agg_s[1, i] - CR * lane
        hit = (off >= 0) & (off < CR)
        held = jnp.where(hit, i, held)
        tag = jnp.where(hit, off + 1, tag)
    tabs[x] = jnp.where(sub == 0, held, tag)
    for o in range(1, NX):
        go(copy(tabs.at[x], tabs.at[x], tab_send.at[NY + o], tab_recv.at[NY + o], x_dev(o)))

    def name_pairs():
        got_cols.wait()
        got_lengths.wait()

        def name(i, both):
            for k in range(KA):
                off = jnp.where(k < lengths_s[0, i], cols_s[k, i], 0) - FR - 2 * lane
                both = tuple(jnp.where(off == c, 1, both[c]) for c in range(2))
            return both

        none = jnp.zeros((8, LANES), I32)
        named = lax.fori_loop(0, FR, name, (none, none))
        tabs[NX] = named[0] * named[1]

    def cut_blocks(leg):
        @pl.loop(FR * leg // 3, FR * (leg + 1) // 3)
        def _(i):
            for k in range(KA):
                high, low = split(blocks[i * KA + k])
                cut[i * KA + k] = jnp.concatenate([high, low], axis=1)

    def pick(o, put):
        dest = rid(y, (x + o // NC) % NX, (core + o % NC) % NC)
        extra_y, extra_row = 0, 0
        for yy in range(NY):
            first, second = plans_s[yy, 0, dest], plans_s[yy, 1, dest]
            put(yy, column[yy, jnp.where(first >= 0, first, jnp.maximum(second, 0))])
            both = jnp.minimum(first, second) >= 0
            extra_y = jnp.where(both, yy, extra_y)
            extra_row = jnp.where(both, second, extra_row)
        put(NY, column[extra_y, extra_row])

    def g_copy(o, src, h):
        return copy(src, pool.at[pl.ds(FR + h * per, per)], g_send.at[o], g_recv.at[o], g_dev(o))

    for step in range(y_steps):
        advance(yr, y_ids, step)
        if step < z_steps - 1:
            advance(zr, z_ids, step)
        if step == 0:
            name_pairs()
        if step == y_steps - 2:
            got_fine.wait()
            cut_blocks(0)
    if y_steps < 2:
        got_fine.wait()
        cut_blocks(0)
    for o in range(1, NY):
        at = plans.at[(y - o + NY) % NY]
        copy(at, at, tab_send.at[o], tab_recv.at[o], y_dev(o)).wait_recv()
    plans_in = bring(1, plans, plans_s)
    plans_in.wait()
    for o in list(range(1, group)) + [0]:
        if o:
            def put(n, v, o=o):
                picked[o, n] = v
        else:
            def put(n, v):
                pool[FR + here * per + n] = v
        pick(o, put)
        if o:
            go(g_copy(o, picked.at[o], here))
    z_next = min(y_steps, z_steps - 1)
    for leg in (1, 2):
        if z_next < z_steps - 1:
            advance(zr, z_ids, z_next)
            z_next += 1
        cut_blocks(leg)
    for o in range(1, NX):
        at = tabs.at[(x - o + NX) % NX]
        copy(at, at, tab_send.at[NY + o], tab_recv.at[NY + o], x_dev(o)).wait_recv()
    tabs_in = bring(2, tabs, tabs_s)

    got_coarse.wait()
    while z_next < z_steps - 1:
        advance(zr, z_ids, z_next)
        z_next += 1
    tabs_in.wait()
    for o in range(1, group):
        src = ((x - o // NC + NX) % NX) * NC + (core - o % NC + NC) % NC
        g_copy(o, pool.at[pl.ds(FR + src * per, per)], src).wait_recv()

    r8 = lax.broadcasted_iota(I32, (KC * A8, LANES), 0)
    l8 = lax.broadcasted_iota(I32, (KC * A8, LANES), 1)
    same_a = (r8 % A8) == (l8 % A8)
    slot_row = lax.broadcasted_iota(I32, (KC, A8, LANES), 0)
    lane_ks = lane // A8

    def couple(i):
        for k in range(KA):
            c = cols_s[k, i]
            ghost = jnp.maximum(c - FR, 0)
            q, odd = lax.div(ghost, 2), lax.rem(ghost, 2)
            slot = lax.div(q, group)
            slot = jnp.where(odd * tabs_s[NX, 0, q] > 0, NY, slot)
            at = jnp.where(c < FR, c, FR + lax.rem(q, group) * per + slot)
            lhs = wide(pool[at].reshape(2 * A8, LANES))
            both = lax.dot_general(lhs, cut[i * KA + k], NT, preferred_element_type=F32)
            applied[i, 2 * A8 * k:2 * A8 * (k + 1)] = both[:2 * A8] + both[2 * A8:]
        applied[i, 2 * A8 * KA:] = jnp.zeros((LANES - 2 * A8 * KA, LANES), F32)
        xh, xl = split(applied[i])
        rhs = jnp.concatenate([xh, xl], axis=0)
        for t in range(2):
            v = jnp.full((8, LANES), -1, I32)
            for k in range(KA):
                for s in range(2):
                    slot = jnp.where(k < lengths_s[0, i], coarse_s[t, k, s, i], -1)
                    v = jnp.where(lane_ks == 2 * k + s, slot, v)
            hit = (v[None] == slot_row).reshape(KC * A8, LANES) & same_a
            where = jnp.where(hit, 1.0, 0.0).astype(BF16)
            summed = lax.dot_general(
                jnp.concatenate([where, where], axis=1), rhs, NN, preferred_element_type=F32
            )
            wided[i, t] = wide(summed)

    def product(i, t):
        high, low = split(whole[:, i, t].reshape(NB, LANES))
        both = lax.dot_general(
            wided[i, t], jnp.concatenate([high, low], axis=1), NT, preferred_element_type=F32
        )
        return (both[:KC * A8] + both[KC * A8:]).reshape(KC, A8, NB)

    @pl.loop(0, FR)
    def _(i):
        couple(i)

    advance(zr, z_ids, z_steps - 1)

    @pl.loop(0, FR)
    def _(i):
        made = product(i, 1)
        for stage in range(STAGES):
            far[stage][x, i] = made[stage * EC:(stage + 1) * EC]

    def x_copy(stage, o, at):
        n = stage * NX + o
        return copy(far[stage].at[at], far[stage].at[at], x_send.at[n], x_recv.at[n], x_dev(o))

    def x_start(stage):
        for o in range(1, NX):
            if stage:
                x_copy(stage - 1, o, x).wait_send()
            x_copy(stage, o, x).start()

    def x_wait(stage):
        for o in range(1, NX):
            x_copy(stage, o, (x - o + NX) % NX).wait_recv()

    def c_copy(stage):
        return copy(
            acc.at[(core + 1) % NC, stage], crossed.at[stage], c_send.at[stage], c_recv.at[stage], core_dev
        )

    def combine(stage):
        for cc in range(NC):
            @pl.loop(0, NY)
            def _(yy):
                dest = rid(yy, x, cc)
                sums = [jnp.zeros((EC, A8, NB), F32) for _ in range(CR)]
                for xx in range(NX):
                    rows = far[stage][xx, tabs_s[xx, 0, dest]]
                    tag = tabs_s[xx, 1, dest]
                    for c in range(CR):
                        sums[c] += rows * jnp.where(tag == c + 1, 1.0, 0.0)
                for c in range(CR):
                    acc[cc, stage, yy, c] = sums[c]

        go(c_copy(stage))

    def r_copy(stage, o):
        n = stage * NY + o
        return copy(
            crossed.at[stage, (y + o) % NY], running.at[stage, o], r_send.at[n], r_recv.at[n], y_dev(o)
        )

    def r_start(stage):
        c_copy(stage).wait_recv()
        for o in sorted(range(1, NY), key=lambda o: -min(o, NY - o)):
            crossed[stage, (y + o) % NY] += acc[core, stage, (y + o) % NY]
            go(r_copy(stage, o))

    def finish(stage):
        total = own[:, stage * EC:(stage + 1) * EC] + crossed[stage, y] + acc[core, stage, y]
        for o in range(1, NY):
            r_copy(stage, o).wait_recv()
            total += running[stage, o]
        out[:, stage * EC:(stage + 1) * EC] = total

    x_start(0)
    own[...] = jnp.zeros_like(own)

    @pl.loop(0, FR)
    def _(i):
        made = product(i, 0)
        for c in range(CR):
            own[c] += made * jnp.where(agg_s[0, i] == row * CR + c, 1.0, 0.0)

    x_start(1)
    for stage in range(STAGES):
        x_wait(stage)
        if stage + 2 < STAGES:
            x_start(stage + 2)
        combine(stage)
        r_start(stage)
    for stage in range(STAGES):
        finish(stage)
    for o in range(1, NX):
        x_copy(STAGES - 1, o, x).wait_send()

    for c in sent:
        c.wait_send()


def per_device(fine_blocks, block_cols, row_length, prolong, aggregates, coarse_slot, send_plan):
    peers, NZ = lax.axis_size("rows"), lax.axis_size("cols")
    FR, KA = fine_blocks.shape[:2]
    group = NX * NC
    NY = peers // group
    per = NY + 1
    NB = NZ * A8
    EC = KC // STAGES

    hbm = pl.BlockSpec(memory_space=pltpu.HBM)
    count_z, count_y = len(ring_ids(NZ, HALVES)), len(ring_ids(NY, HALVES))
    dma = pltpu.SemaphoreType.DMA
    return pl.pallas_call(
        functools.partial(kernel, (NY, NZ, FR, KA)),
        out_shape=jax.ShapeDtypeStruct((CR, KC, A8, NB), F32),
        in_specs=[hbm] * 7,
        out_specs=pl.BlockSpec(memory_space=pltpu.VMEM),
        scratch_shapes=[
            pltpu.VMEM((FR * KA, LANES, LANES), F32),
            pltpu.VMEM((FR * KA, LANES, 2 * LANES), BF16),
            pltpu.VMEM((NZ, FR, 2, A8, LANES), F32),
            pltpu.VMEM((NY, FR, 2, A8, LANES), F32),
            pltpu.VMEM((NY, 2, peers), I32),
            pltpu.SMEM((NY, 2, peers), I32),
            pltpu.VMEM((NX + 1, 8, LANES), I32),
            pltpu.SMEM((NX + 1, 8, LANES), I32),
            pltpu.SMEM((KA, FR), I32),
            pltpu.SMEM((1, FR), I32),
            pltpu.SMEM((2, FR), I32),
            pltpu.SMEM((2, KA, 2, FR), I32),
            pltpu.VMEM((group, per, 2, A8, LANES), F32),
            pltpu.VMEM((FR + group * per, 2, A8, LANES), F32),
            pltpu.VMEM((FR, LANES, LANES), F32),
            pltpu.VMEM((FR, 2, 2 * KC * A8, 2 * LANES), BF16),
            *[pltpu.VMEM((NX, FR, EC, A8, NB), F32) for _ in range(STAGES)],
            pltpu.VMEM((CR, KC, A8, NB), F32),
            pltpu.VMEM((NC, STAGES, NY, CR, EC, A8, NB), F32),
            pltpu.VMEM((STAGES, NY, CR, EC, A8, NB), F32),
            pltpu.VMEM((STAGES, NY, CR, EC, A8, NB), F32),
            dma((7,)), dma((NY + NX,)), dma((NY + NX,)), dma((count_z,)), dma((count_z,)),
            dma((count_y,)), dma((count_y,)), dma((group,)), dma((group,)),
            dma((STAGES * NX,)), dma((STAGES * NX,)), dma((STAGES,)), dma((STAGES,)),
            dma((STAGES * NY,)), dma((STAGES * NY,)),
        ],
        compiler_params=pltpu.CompilerParams(
            collective_id=0, has_side_effects=True, vmem_limit_bytes=56 * 2**20
        ),
    )(
        fine_blocks.reshape(FR * KA, LANES, LANES), prolong, block_cols.T, row_length[None, :], aggregates.T,
        jnp.transpose(coarse_slot, (1, 2, 3, 0)), jnp.transpose(send_plan[0]),
    )


def solution(mesh):
    return jax.shard_map(
        per_device,
        mesh=mesh,
        in_specs=(
            P("rows", None, None, None),
            P("rows", None),
            P("rows"),
            P("rows", None, "cols", None),
            P("rows", None),
            P("rows", None, None, None),
            P("rows", None, None),
        ),
        out_specs=P("rows", None, "cols", None),
        check_vma=False,
    )
```

```python
import functools

import jax
import jax.numpy as jnp
from jax import lax
from jax.experimental import pallas as pl
from jax.experimental.pallas import tpu as pltpu
from jax.sharding import PartitionSpec as P

NX, NC = 4, 2
KC = 8
CR = 3
A8 = 8
LANES = 128
HALVES = 2
STAGES = 4
UNROLL = 3
F32, BF16, I32 = jnp.float32, jnp.bfloat16, jnp.int32
NT = (((1,), (1,)), ((), ()))
NN = (((1,), (0,)), ((), ()))
MESH = pl.DeviceIdType.MESH


def split(v):
    high = v.astype(BF16)
    return high, (v - high.astype(F32)).astype(BF16)


def wide(v):
    high, low = split(v)
    return jnp.concatenate(
        [jnp.concatenate([high, high], axis=1), jnp.concatenate([low, jnp.zeros_like(low)], axis=1)], axis=0
    )


def steps_of(count, half):
    plus = count // 2 if half % 2 == 0 else count // 2 - 1
    return plus, count - 1 - plus


def ring_ids(count, halves):
    ids = {}
    for half in range(halves):
        for way, steps in zip((1, -1), steps_of(count, half)):
            for step in range(steps):
                ids[half, way, step] = len(ids)
    return ids


def kernel(
    dims, fine, prolong, cols, lengths, agg, coarse, plan, out,
    blocks, cut, whole, column, plans, plans_s, tabs, tabs_s, cols_s, lengths_s, agg_s, coarse_s,
    picked, pool, applied, wided, far_a, far_b, far_c, far_d, own, acc, crossed, running,
    local_sem, tab_send, tab_recv, z_send, z_recv, y_send, y_recv, g_send, g_recv,
    x_send, x_recv, c_send, c_recv, r_send, r_recv,
):
    NY, NZ, FR, KA = dims
    group = NX * NC
    per = NY + 1
    NB = NZ * A8
    EC = KC // STAGES
    hr = FR // HALVES
    y_steps, z_steps = NY // 2, NZ // 2
    far = (far_a, far_b, far_c, far_d)
    row, z = lax.axis_index("rows"), lax.axis_index("cols")
    core, x, y = row % NC, (row // NC) % NX, row // group
    here = x * NC + core

    def rid(yy, xx, cc):
        return (yy * NX + xx) * NC + cc

    def copy(src, dst, send, recv, device):
        return pltpu.make_async_remote_copy(
            src_ref=src, dst_ref=dst, send_sem=send, recv_sem=recv, device_id=device, device_id_type=MESH
        )

    def z_dev(way):
        return (row, (z + way + NZ) % NZ)

    def y_dev(way):
        return (rid((y + way + NY) % NY, x, core), z)

    def x_dev(way):
        return (rid(y, (x + way + NX) % NX, core), z)

    def g_dev(o):
        return (rid(y, (x + o // NC) % NX, (core + o % NC) % NC), z)

    core_dev = (rid(y, x, (core + 1) % NC), z)

    def bring(n, src, dst):
        c = pltpu.make_async_copy(src, dst, local_sem.at[n])
        c.start()
        return c

    got_rows = bring(0, prolong, column.at[y])
    got_sides = [bring(7 + t, prolong.at[:, t], whole.at[t, z]) for t in range(2)]
    got_plan = bring(1, plan, plans.at[y])
    got_agg = bring(2, agg, agg_s)
    got_cols = bring(3, cols, cols_s)
    got_lengths = bring(4, lengths, lengths_s)
    got_coarse = bring(5, coarse, coarse_s)
    got_fine = bring(6, fine, blocks)

    barrier = pltpu.get_barrier_semaphore()
    partners = [z_dev(o) for o in sorted({1, 2, NZ - 2, NZ - 1} - {0, NZ})]
    partners += [y_dev(o) for o in range(1, NY)]
    partners += [g_dev(o) for o in range(1, group)]
    for device in partners:
        pl.semaphore_signal(barrier, inc=1, device_id=device, device_id_type=MESH)
    got_rows.wait()
    for c in got_sides:
        c.wait()
    got_plan.wait()
    pl.semaphore_wait(barrier, len(partners))

    sent = []

    def go(c):
        c.start()
        sent.append(c)

    y_ids = ring_ids(NY, HALVES)

    def rows_of(half):
        return pl.ds(half * hr, hr)

    def ring_send(buf, ids, send, recv, me, count, dev, half, way, step):
        at = (me - way * step + count) % count
        part = buf.at[at, rows_of(half)]
        n = ids[half, way, step]
        go(copy(part, part, send.at[n], recv.at[n], dev(way)))

    def ring_wait(buf, ids, send, recv, me, count, dev, half, way, step):
        at = (me - way * (step + 1) + 2 * count) % count
        part = buf.at[at, rows_of(half)]
        n = ids[half, way, step]
        copy(part, part, send.at[n], recv.at[n], dev(way)).wait_recv()

    yr = (column, y_ids, y_send, y_recv, y, NY, y_dev)

    def advance(ring, ids, step):
        for half in range(HALVES):
            for way in (1, -1):
                if (half, way, step) in ids:
                    ring_wait(*ring, half, way, step)
                    if (half, way, step + 1) in ids:
                        ring_send(*ring, half, way, step + 1)

    for half in range(HALVES):
        for way in (1, -1):
            if (half, way, 0) in y_ids:
                ring_send(*yr, half, way, 0)
    z_reach = {(t, way): steps_of(NZ, t)[0 if way == 1 else 1] for t in range(2) for way in (1, -1)}
    z_ids = {}
    for t, way in z_reach:
        for far_by in range(1, z_reach[t, way] + 1):
            z_ids[t, way, far_by] = len(z_ids)

    def z_copy(t, way, far_by, at):
        n = z_ids[t, way, far_by]
        part = whole.at[t, at]
        return copy(part, part, z_send.at[n], z_recv.at[n], z_dev(way * (1 if far_by % 2 else 2)))

    def z_push(t, base):
        for hop in (2, 1):
            for way in (1, -1):
                if base + hop <= z_reach[t, way]:
                    go(z_copy(t, way, base + hop, (z - way * base + NZ) % NZ))

    def z_wait(t, far_by):
        for way in (1, -1):
            if far_by <= z_reach[t, way]:
                z_copy(t, way, far_by, (z - way * far_by + NZ) % NZ).wait_recv()

    def z_step(t, base):
        z_wait(t, base)
        z_push(t, base)

    def z_rest(t):
        for far_by in range(1, z_steps + 1):
            if far_by % 2 or far_by == z_steps:
                z_wait(t, far_by)

    relays = list(range(2, z_steps, 2))
    queue = []
    for n, base in enumerate(relays):
        queue += [(1, base)] + [(0, b) for b in relays[n - 1:n] if n]
    queue += [(0, b) for b in relays[-1:]]

    def z_next():
        if queue:
            z_step(*queue.pop(0))

    z_push(1, 0)
    for o in range(1, NY):
        go(copy(plans.at[y], plans.at[y], tab_send.at[o], tab_recv.at[o], y_dev(o)))
    pool[pl.ds(0, FR)] = column[y]

    lane = lax.broadcasted_iota(I32, (8, LANES), 1)
    sub = lax.broadcasted_iota(I32, (8, LANES), 0)
    got_agg.wait()
    held = jnp.zeros((8, LANES), I32)
    tag = jnp.zeros((8, LANES), I32)
    for i in range(FR):
        off = agg_s[1, i] - CR * lane
        hit = (off >= 0) & (off < CR)
        held = jnp.where(hit, i, held)
        tag = jnp.where(hit, off + 1, tag)
    tabs[x] = jnp.where(sub == 0, held, tag)
    for o in range(1, NX):
        go(copy(tabs.at[x], tabs.at[x], tab_send.at[NY + o], tab_recv.at[NY + o], x_dev(o)))

    def name_pairs():
        got_cols.wait()
        got_lengths.wait()

        def name(i, both):
            for k in range(KA):
                off = jnp.where(k < lengths_s[0, i], cols_s[k, i], 0) - FR - 2 * lane
                both = tuple(jnp.where(off == c, 1, both[c]) for c in range(2))
            return both

        none = jnp.zeros((8, LANES), I32)
        named = lax.fori_loop(0, FR, name, (none, none))
        tabs[NX] = named[0] * named[1]

    def cut_blocks(leg):
        @pl.loop(FR * leg // 3, FR * (leg + 1) // 3)
        def _(i):
            for k in range(KA):
                high, low = split(blocks[i * KA + k])
                cut[i * KA + k] = jnp.concatenate([high, low], axis=1)

    def pick(o, put):
        dest = rid(y, (x + o // NC) % NX, (core + o % NC) % NC)
        extra_y, extra_row = 0, 0
        for yy in range(NY):
            first, second = plans_s[yy, 0, dest], plans_s[yy, 1, dest]
            put(yy, column[yy, jnp.where(first >= 0, first, jnp.maximum(second, 0))])
            both = jnp.minimum(first, second) >= 0
            extra_y = jnp.where(both, yy, extra_y)
            extra_row = jnp.where(both, second, extra_row)
        put(NY, column[extra_y, extra_row])

    def g_copy(o, src, h):
        return copy(src, pool.at[pl.ds(FR + h * per, per)], g_send.at[o], g_recv.at[o], g_dev(o))

    for step in range(y_steps):
        advance(yr, y_ids, step)
        z_next()
        if step == 0:
            z_push(0, 0)
            name_pairs()
        if step == y_steps - 2:
            got_fine.wait()
            cut_blocks(0)
    if y_steps < 2:
        got_fine.wait()
        cut_blocks(0)
    for o in range(1, NY):
        at = plans.at[(y - o + NY) % NY]
        copy(at, at, tab_send.at[o], tab_recv.at[o], y_dev(o)).wait_recv()
    plans_in = bring(1, plans, plans_s)
    plans_in.wait()
    for o in list(range(1, group)) + [0]:
        if o:
            def put(n, v, o=o):
                picked[o, n] = v
        else:
            def put(n, v):
                pool[FR + here * per + n] = v
        pick(o, put)
        if o:
            go(g_copy(o, picked.at[o], here))
    cut_blocks(1)
    z_next()
    cut_blocks(2)
    for o in range(1, NX):
        at = tabs.at[(x - o + NX) % NX]
        copy(at, at, tab_send.at[NY + o], tab_recv.at[NY + o], x_dev(o)).wait_recv()
    tabs_in = bring(2, tabs, tabs_s)

    got_coarse.wait()
    while queue:
        z_next()
    tabs_in.wait()
    for o in range(1, group):
        src = ((x - o // NC + NX) % NX) * NC + (core - o % NC + NC) % NC
        g_copy(o, pool.at[pl.ds(FR + src * per, per)], src).wait_recv()

    r8 = lax.broadcasted_iota(I32, (KC * A8, LANES), 0)
    l8 = lax.broadcasted_iota(I32, (KC * A8, LANES), 1)
    same_a = (r8 % A8) == (l8 % A8)
    slot_row = lax.broadcasted_iota(I32, (KC, A8, LANES), 0)
    lane_ks = lane // A8

    def couple(i):
        for k in range(KA):
            c = cols_s[k, i]
            ghost = jnp.maximum(c - FR, 0)
            q, odd = lax.div(ghost, 2), lax.rem(ghost, 2)
            slot = lax.div(q, group)
            slot = jnp.where(odd * tabs_s[NX, 0, q] > 0, NY, slot)
            at = jnp.where(c < FR, c, FR + lax.rem(q, group) * per + slot)
            lhs = wide(pool[at].reshape(2 * A8, LANES))
            both = lax.dot_general(lhs, cut[i * KA + k], NT, preferred_element_type=F32)
            applied[i, 2 * A8 * k:2 * A8 * (k + 1)] = both[:2 * A8] + both[2 * A8:]
        applied[i, 2 * A8 * KA:] = jnp.zeros((LANES - 2 * A8 * KA, LANES), F32)
        xh, xl = split(applied[i])
        rhs = jnp.concatenate([xh, xl], axis=0)
        for t in range(2):
            v = jnp.full((8, LANES), -1, I32)
            for k in range(KA):
                for s in range(2):
                    slot = jnp.where(k < lengths_s[0, i], coarse_s[t, k, s, i], -1)
                    v = jnp.where(lane_ks == 2 * k + s, slot, v)
            hit = (v[None] == slot_row).reshape(KC * A8, LANES) & same_a
            where = jnp.where(hit, 1.0, 0.0).astype(BF16)
            summed = lax.dot_general(
                jnp.concatenate([where, where], axis=1), rhs, NN, preferred_element_type=F32
            )
            wided[i, t] = wide(summed)

    def product(i, t):
        high, low = split(whole[t, :, i].reshape(NB, LANES))
        both = lax.dot_general(
            wided[i, t], jnp.concatenate([high, low], axis=1), NT, preferred_element_type=F32
        )
        return (both[:KC * A8] + both[KC * A8:]).reshape(KC, A8, NB)

    @pl.loop(0, FR, unroll=UNROLL)
    def _(i):
        couple(i)

    z_rest(1)

    @pl.loop(0, FR, unroll=UNROLL)
    def _(i):
        made = product(i, 1)
        for stage in range(STAGES):
            far[stage][x, i] = made[stage * EC:(stage + 1) * EC]

    def x_copy(stage, o, at):
        n = stage * NX + o
        return copy(far[stage].at[at], far[stage].at[at], x_send.at[n], x_recv.at[n], x_dev(o))

    def x_start(stage):
        for o in range(1, NX):
            x_copy(stage, o, x).start()

    def x_wait(stage):
        for o in range(1, NX):
            x_copy(stage, o, (x - o + NX) % NX).wait_recv()

    def c_copy(stage):
        return copy(
            acc.at[(core + 1) % NC, stage], crossed.at[stage], c_send.at[stage], c_recv.at[stage], core_dev
        )

    def combine(stage):
        for cc in range(NC):
            @pl.loop(0, NY)
            def _(yy):
                dest = rid(yy, x, cc)
                sums = [jnp.zeros((EC, A8, NB), F32) for _ in range(CR)]
                for xx in range(NX):
                    rows = far[stage][xx, tabs_s[xx, 0, dest]]
                    tag = tabs_s[xx, 1, dest]
                    for c in range(CR):
                        sums[c] += rows * jnp.where(tag == c + 1, 1.0, 0.0)
                for c in range(CR):
                    acc[cc, stage, yy, c] = sums[c]

        go(c_copy(stage))

    def r_copy(stage, o):
        n = stage * NY + o
        return copy(
            crossed.at[stage, (y + o) % NY], running.at[stage, o], r_send.at[n], r_recv.at[n], y_dev(o)
        )

    def r_start(stage):
        c_copy(stage).wait_recv()
        for o in sorted(range(1, NY), key=lambda o: -min(o, NY - o)):
            crossed[stage, (y + o) % NY] += acc[core, stage, (y + o) % NY]
            go(r_copy(stage, o))

    def finish(stage):
        total = own[:, stage * EC:(stage + 1) * EC] + crossed[stage, y] + acc[core, stage, y]
        for o in range(1, NY):
            r_copy(stage, o).wait_recv()
            total += running[stage, o]
        out[:, stage * EC:(stage + 1) * EC] = total

    def own_products():
        own[...] = jnp.zeros_like(own)
        z_rest(0)

        @pl.loop(0, FR)
        def _(i):
            made = product(i, 0)
            for c in range(CR):
                own[c] += made * jnp.where(agg_s[0, i] == row * CR + c, 1.0, 0.0)

    x_start(0)
    own_products()
    x_start(1)
    for stage in range(STAGES):
        x_wait(stage)
        if stage + 2 < STAGES:
            x_start(stage + 2)
        combine(stage)
        r_start(stage)
    for stage in range(STAGES):
        finish(stage)
    for stage in range(STAGES):
        for o in range(1, NX):
            x_copy(stage, o, x).wait_send()

    for c in sent:
        c.wait_send()


def per_device(fine_blocks, block_cols, row_length, prolong, aggregates, coarse_slot, send_plan):
    peers, NZ = lax.axis_size("rows"), lax.axis_size("cols")
    FR, KA = fine_blocks.shape[:2]
    group = NX * NC
    NY = peers // group
    per = NY + 1
    NB = NZ * A8
    EC = KC // STAGES

    hbm = pl.BlockSpec(memory_space=pltpu.HBM)
    count_z, count_y = 2 * (NZ - 1), len(ring_ids(NY, HALVES))
    dma = pltpu.SemaphoreType.DMA
    return pl.pallas_call(
        functools.partial(kernel, (NY, NZ, FR, KA)),
        out_shape=jax.ShapeDtypeStruct((CR, KC, A8, NB), F32),
        in_specs=[hbm] * 7,
        out_specs=pl.BlockSpec(memory_space=pltpu.VMEM),
        scratch_shapes=[
            pltpu.VMEM((FR * KA, LANES, LANES), F32),
            pltpu.VMEM((FR * KA, LANES, 2 * LANES), BF16),
            pltpu.VMEM((2, NZ, FR, A8, LANES), F32),
            pltpu.VMEM((NY, FR, 2, A8, LANES), F32),
            pltpu.VMEM((NY, 2, peers), I32),
            pltpu.SMEM((NY, 2, peers), I32),
            pltpu.VMEM((NX + 1, 8, LANES), I32),
            pltpu.SMEM((NX + 1, 8, LANES), I32),
            pltpu.SMEM((KA, FR), I32),
            pltpu.SMEM((1, FR), I32),
            pltpu.SMEM((2, FR), I32),
            pltpu.SMEM((2, KA, 2, FR), I32),
            pltpu.VMEM((group, per, 2, A8, LANES), F32),
            pltpu.VMEM((FR + group * per, 2, A8, LANES), F32),
            pltpu.VMEM((FR, LANES, LANES), F32),
            pltpu.VMEM((FR, 2, 2 * KC * A8, 2 * LANES), BF16),
            *[pltpu.VMEM((NX, FR, EC, A8, NB), F32) for _ in range(STAGES)],
            pltpu.VMEM((CR, KC, A8, NB), F32),
            pltpu.VMEM((NC, STAGES, NY, CR, EC, A8, NB), F32),
            pltpu.VMEM((STAGES, NY, CR, EC, A8, NB), F32),
            pltpu.VMEM((STAGES, NY, CR, EC, A8, NB), F32),
            dma((9,)), dma((NY + NX,)), dma((NY + NX,)), dma((count_z,)), dma((count_z,)),
            dma((count_y,)), dma((count_y,)), dma((group,)), dma((group,)),
            dma((STAGES * NX,)), dma((STAGES * NX,)), dma((STAGES,)), dma((STAGES,)),
            dma((STAGES * NY,)), dma((STAGES * NY,)),
        ],
        compiler_params=pltpu.CompilerParams(
            collective_id=0, has_side_effects=True, vmem_limit_bytes=56 * 2**20
        ),
    )(
        fine_blocks.reshape(FR * KA, LANES, LANES), prolong, block_cols.T, row_length[None, :], aggregates.T,
        jnp.transpose(coarse_slot, (1, 2, 3, 0)), jnp.transpose(send_plan[0]),
    )


def solution(mesh):
    return jax.shard_map(
        per_device,
        mesh=mesh,
        in_specs=(
            P("rows", None, None, None),
            P("rows", None),
            P("rows"),
            P("rows", None, "cols", None),
            P("rows", None),
            P("rows", None, None, None),
            P("rows", None, None),
        ),
        out_specs=P("rows", None, "cols", None),
        check_vma=False,
    )
```
